32 devices in a mesh: row: 8 (over z, x), col: 4 (over y, core).
Axes of the slice: x: 2, y: 2, z: 4, core: 2. Of those that a mesh axis runs over, the one named last changes fastest.
Arguments:
- arriving: float32 [16384, 256], P(('row', 'col')), may hold values from -0.6 to 0.6
- expiring: float32 [16384, 256], P(('row', 'col')), may hold values from -0.6 to 0.6
- taps: float32 [9], replicated, may hold values from -1.4 to 1.4
- covariance: float32 [16384, 16384], P('row', 'col'), may hold values from -1 to 6, as said below
- vectors: float32 [16384, 256], P(('row', 'col')), may hold values from -6 to 6
Outputs:
- updated: float32 [16384, 16384], P('row', 'col')
- basis: float32 [16384, 256], P(('row', 'col'))
The draws below stay inside these ranges and needn't reach their ends.
Inputs may be any that keep to these rules, and one draw needn't show every extreme that they name: `covariance`: symmetric.
All inputs are finite; a program needn't handle non-finite values.
Results may differ from the reference program's by a relative error of at most 0.0013.
Values may be sent and summed in bfloat16 or wider, within the bound.
No kernel may reach another device: no remote copies, remote signals or barrier semaphores. Data moves between devices by JAX's collectives and lax.ppermute only.
A program may use at most 192 MiB of HBM per device.

```python
import math
import jax
import jax.numpy as jnp
from jax import lax

CH = 16384
SAMPLES = 256
K = 256
TAPS = 9
HALF = 4


def draw_covariance(key, part):
    noise_key, level_key = jax.random.split(key)
    noise = jnp.clip(jax.random.normal(noise_key, (CH, CH), jnp.float32), -6.0, 6.0)
    coupled = (noise + noise.T) * (0.5 / math.sqrt(2.0 * CH))
    levels = jax.random.uniform(level_key, (CH,), jnp.float32, 2.0, 6.0)
    places = jnp.arange(CH)
    return jnp.where(places[:, None] == places[None, :], levels[:, None], coupled)


def shard_levels(rng, dims, cuts, least, largest):
    factor_of, own = 1.0, jax.random.fold_in(rng, 6)
    for position, blocks in cuts:
        draws = jnp.exp(jax.random.uniform(jax.random.fold_in(own, position), (blocks,), jnp.float32, least / len(cuts), largest / len(cuts)))
        factor_of = factor_of * jnp.repeat(draws, dims[position] // blocks).reshape([-1 if axis == position else 1 for axis in range(len(dims))])
    return factor_of


def gaussian(key, dims, width, bound, shards=(), dtype=jnp.bfloat16):
    level = shard_levels(key, dims, shards, -0.22, 0.18) if shards else 1.0
    result = jax.random.normal(key, dims, jnp.float32) * width * level
    return jnp.minimum(jnp.maximum(result, -bound), bound).astype(dtype)


def setup_inputs(seed: int = 0) -> dict:
    splits = jax.random.split(jax.random.key(seed), 6)
    return {
        "arriving": gaussian(splits[0], (CH, SAMPLES), 0.1, 0.6, ((0, 32),), jnp.float32),
        "expiring": gaussian(splits[1], (CH, SAMPLES), 0.1, 0.6, ((0, 32),), jnp.float32),
        "taps": gaussian(splits[2], (TAPS,), 0.35, 1.4, (), jnp.float32),
        "covariance": draw_covariance(jax.random.fold_in(splits[5], 71), 0),
        "vectors": gaussian(splits[4], (CH, K), 1.0, 6.0, ((0, 32),), jnp.float32),
    }


def spatial_filter(raw, taps):
    padded = jnp.pad(raw, ((HALF, HALF), (0, 0)))
    total = jnp.zeros(raw.shape, jnp.float32)
    for tap in range(TAPS):
        total = total + taps[tap] * padded[tap:tap + CH]
    return total.astype(jnp.bfloat16)

def reference(arriving, expiring, taps, covariance, vectors):
    raw = jnp.concatenate([arriving, expiring], 1)
    filtered = spatial_filter(raw, taps)
    widened = filtered.astype(jnp.float32)
    signed = jnp.concatenate([widened[:, :SAMPLES], -widened[:, SAMPLES:]], 1)
    change = jnp.dot(widened, signed.T, precision=lax.Precision.HIGHEST) / SAMPLES
    updated = covariance + change
    first = jnp.dot(updated, vectors, precision=lax.Precision.HIGHEST)
    second = jnp.dot(updated, first, precision=lax.Precision.HIGHEST)
    gram = jnp.dot(second.T, second, precision=lax.Precision.HIGHEST) / CH
    factor = jnp.linalg.cholesky(gram)
    basis = jax.scipy.linalg.solve_triangular(factor, second.T, lower=True).T
    return (updated, basis)
```

```python
import functools
import math

import jax
import jax.numpy as jnp
from jax import lax
from jax.experimental import pallas as pl
from jax.experimental.pallas import tpu as pltpu
from jax.sharding import PartitionSpec as P

HIGHEST = lax.Precision.HIGHEST
F32, F16, BF16 = jnp.float32, jnp.float16, jnp.bfloat16
VMEM_LIMIT = 40 * 1024 * 1024


def swap(cells, axis, mask):
    return lax.ppermute(cells, axis, [(i, i ^ mask) for i in range(lax.axis_size(axis))])


def bits_of(axis):
    return [1 << b for b in range(lax.axis_size(axis).bit_length() - 1)]


def is_set(axis, mask):
    return (lax.axis_index(axis) & mask) != 0


def pick(upper, first, second):
    return jnp.where(upper, second, first)


def room(bound):
    return 2.0 ** (15 - math.ceil(math.log2(bound)))


def power_of_two_for(value):
    exponent = jnp.floor(jnp.log2(jnp.maximum(value, 1e-30)))
    return lax.reduce_precision(jnp.exp2(-exponent - 1.0), 8, 3)


def after(values, earlier):
    corner = lax.slice(earlier, (0,) * earlier.ndim, (1,) * earlier.ndim)
    entry = corner.reshape(()).astype(F32)
    return values + jnp.where(jnp.isnan(entry), 1, 0).astype(values.dtype)


def gather_pairs(cells, axis):
    blocks = {0: cells}
    for mask in reversed(bits_of(axis)):
        for known in list(blocks):
            blocks[known | mask] = swap(blocks[known], axis, mask)
    return [blocks[mask] for mask in range(lax.axis_size(axis))]


def scatter_sum(cells):
    for mask in bits_of("col"):
        half = cells.shape[0] // 2
        upper = is_set("col", mask)
        low, high = cells[:half], cells[half:]
        cells = pick(upper, low, high) + swap(pick(upper, high, low), "col", mask)
    return cells


def sum_over_row(cells):
    for mask in bits_of("row"):
        cells = cells + swap(cells, "row", mask)
    return cells


def gather_parts(cells):
    for mask in reversed(bits_of("col")):
        other = swap(cells, "col", mask)
        upper = is_set("col", mask)
        cells = jnp.concatenate([pick(upper, cells, other), pick(upper, other, cells)], 0)
    return cells


def largest_everywhere(value, planes):
    value = jnp.full((8, 128), value)
    for other in [swap(value, "row", 2 * j) for j in range(1, planes)]:
        value = jnp.maximum(value, other)
    value = jnp.maximum(value, swap(value, "row", 1))
    for mask in bits_of("col"):
        value = jnp.maximum(value, swap(value, "col", mask))
    return value


def halves(values):
    high = lax.reduce_precision(values, 8, 7)
    return high.astype(BF16), (values - high).astype(BF16)


def split(values):
    high = values.astype(BF16)
    return high, (values - high.astype(F32)).astype(BF16)


def first_kernel(blocks, place, extra, *refs):
    vectors, tiles = refs[:blocks], refs[blocks : 2 * blocks]
    send, keep = refs[2 * blocks :]
    count = send.shape[0]
    total = None
    for part, tile in zip(vectors, tiles):
        high, low = split(tile[...])
        both = jnp.dot(part[...], high, preferred_element_type=F32)
        rest = jnp.dot(part[:count], low, preferred_element_type=F32)
        term = both[:count] + both[count:] + rest
        total = term if total is None else total + term

    @pl.when(pl.program_id(0) == 0)
    def _():
        send[:, : total.shape[1]] = total
        send[:, total.shape[1] :] = extra[...]

    @pl.when(pl.program_id(0) == 1)
    def _():
        keep[:, : total.shape[1]] = total
        keep[:, total.shape[1] :] = extra[...]


def first_part(vectors, tile, extra, z, x, column, stripe):
    rows = tile.shape[0]
    blocks = len(vectors)
    count = vectors[0].shape[0] // 2
    depth = rows // blocks
    width = extra.shape[1]
    if stripe % 128:
        return first_part_plain(vectors, tile, extra, z, x, column, stripe)
    place = jnp.stack(
        [z * 2 + (1 - x), z * 2 + x] + [column ^ i for i in range(blocks)]
    ).astype(jnp.int32)

    def rows_of(member):
        return lambda i, p: (p[2 + member], p[i])

    shape = (count, stripe + width)
    return pl.pallas_call(
        functools.partial(first_kernel, blocks),
        grid_spec=pltpu.PrefetchScalarGridSpec(
            num_scalar_prefetch=1,
            grid=(2,),
            in_specs=[pl.BlockSpec((count, width), lambda i, p: (0, 0))]
            + [pl.BlockSpec((2 * count, depth), lambda i, p: (0, 0))] * blocks
            + [pl.BlockSpec((depth, stripe), rows_of(i)) for i in range(blocks)],
            out_specs=[pl.BlockSpec(shape, lambda i, p: (0, 0))] * 2,
        ),
        out_shape=[jax.ShapeDtypeStruct(shape, F32)] * 2,
        compiler_params=pltpu.CompilerParams(vmem_limit_bytes=VMEM_LIMIT),
        cost_estimate=pl.CostEstimate(
            flops=12 * count * rows * stripe, bytes_accessed=8 * rows * stripe, transcendentals=0
        ),
        name="first_part",
    )(place, extra, *vectors, *([tile] * blocks))


def first_part_plain(vectors, tile, extra, z, x, column, stripe):
    count = vectors[0].shape[0] // 2
    depth = tile.shape[0] // len(vectors)
    results = []
    for other in (1 - x, x):
        total = 0.0
        for i, part in enumerate(vectors):
            start = ((column ^ i) * depth, (z * 2 + other) * stripe)
            cells = lax.dynamic_slice(tile, start, (depth, stripe))
            values = part[:count].astype(F32) + part[count:].astype(F32)
            total = total + jnp.dot(values, cells, precision=HIGHEST)
        results.append(jnp.concatenate([total, extra], 1))
    return results


def second_part_plain(tile, entries, z, x, before):
    depth = entries[0].shape[0]
    total = 0.0 if before is None else before
    for i, other in enumerate((x, 1 - x)):
        start = (0, (z * 2 + other) * depth)
        cells = lax.dynamic_slice(tile, start, (tile.shape[0], depth))
        values = entries[2 * i].astype(F32) + entries[2 * i + 1].astype(F32)
        total = total + jnp.dot(cells, values, precision=HIGHEST)
    return total


def turn_kernel(cells, out):
    out[...] = cells[...].T


def turned(cells):
    return pl.pallas_call(
        turn_kernel,
        out_shape=jax.ShapeDtypeStruct(cells.shape[::-1], F32),
        compiler_params=pltpu.CompilerParams(vmem_limit_bytes=VMEM_LIMIT),
        name="turned",
    )(cells)


def second_kernel(started, place, *refs):
    tiles, entries = refs[:2], refs[2:6]
    out = refs[-1]
    total = refs[6][...] if started else None
    for tile, top, rest in zip(tiles, entries[::2], entries[1::2]):
        high, low = split(tile[...])
        term = (
            jnp.dot(high, top[...], preferred_element_type=F32)
            + jnp.dot(high, rest[...], preferred_element_type=F32)
            + jnp.dot(low, top[...], preferred_element_type=F32)
        )
        total = term if total is None else total + term
    out[...] = total


def second_part(tile, entries, z, x, before):
    rows = tile.shape[0]
    depth, count = entries[0].shape
    if depth % 128:
        return second_part_plain(tile, entries, z, x, before)
    block = min(rows, 512)
    specs = [
        pl.BlockSpec((block, depth), lambda i, p: (i, p[0])),
        pl.BlockSpec((block, depth), lambda i, p: (i, p[1])),
    ] + [pl.BlockSpec((depth, count), lambda i, p: (0, 0))] * 4
    operands = [tile, tile, *entries]
    total = pl.BlockSpec((block, count), lambda i, p: (i, 0))
    if before is not None:
        specs.append(total)
        operands.append(before)
    return pl.pallas_call(
        functools.partial(second_kernel, before is not None),
        grid_spec=pltpu.PrefetchScalarGridSpec(
            num_scalar_prefetch=1, grid=(rows // block,), in_specs=specs, out_specs=total
        ),
        out_shape=jax.ShapeDtypeStruct((rows, count), F32),
        compiler_params=pltpu.CompilerParams(vmem_limit_bytes=VMEM_LIMIT),
        cost_estimate=pl.CostEstimate(
            flops=12 * count * rows * depth, bytes_accessed=8 * rows * depth, transcendentals=0
        ),
        name="second_part",
    )(jnp.stack([z * 2 + x, z * 2 + (1 - x)]).astype(jnp.int32), *operands)


def update_kernel(scale, tile, rows, columns, *rest):
    change = lax.dot_general(
        rows[...], columns[...], (((1,), (1,)), ((), ())), preferred_element_type=F32
    )
    rest[-1][...] = tile[...] + change * scale


def update_part(tile, rows, columns, part, parts, before, scale):
    height, width = tile.shape
    depth = rows.shape[1]
    high = min(height // parts, 256)
    steps = height // parts // high
    specs = [
        pl.BlockSpec((high, width), lambda i: (part * steps + i, 0)),
        pl.BlockSpec((high, depth), lambda i: (part * steps + i, 0)),
        pl.BlockSpec((width, depth), lambda i: (0, 0)),
    ]
    operands = [tile, rows, columns]
    if before is not None:
        specs.append(pl.BlockSpec(memory_space=pl.ANY))
        operands.append(before)
    return pl.pallas_call(
        functools.partial(update_kernel, scale),
        grid=(steps,),
        in_specs=specs,
        out_specs=pl.BlockSpec((high, width), lambda i: (part * steps + i, 0)),
        out_shape=jax.ShapeDtypeStruct((height, width), F32),
        input_output_aliases={} if before is None else {3: 0},
        compiler_params=pltpu.CompilerParams(vmem_limit_bytes=VMEM_LIMIT),
        cost_estimate=pl.CostEstimate(
            flops=2 * height * width * depth // parts,
            bytes_accessed=8 * height * width // parts,
            transcendentals=0,
        ),
        name="update_part",
    )(*operands)


def filter_kernel(taps, arriving, expiring, above, below, out, work):
    stripe, samples = arriving.shape
    count = taps.shape[0]
    half = count // 2
    work[8 - half : 8, :] = above[...]
    work[8 : 8 + stripe, :samples] = arriving[...]
    work[8 : 8 + stripe, samples:] = expiring[...]
    work[8 + stripe : 8 + stripe + half, :] = below[...]
    step = 64
    for start in range(0, stripe, step):
        total = taps[0] * work[8 - half + start : 8 - half + start + step, :]
        for tap in range(1, count):
            begin = 8 - half + start + tap
            total = total + taps[tap] * work[begin : begin + step, :]
        out[start : start + step, :] = total.astype(BF16)


def filter_stripe(arriving, expiring, taps):
    stripe, samples = arriving.shape
    half = taps.shape[0] // 2
    axes = ("row", "col")
    count = lax.axis_size("row") * lax.axis_size("col")
    head = jnp.concatenate([arriving[:half], expiring[:half]], 1)
    tail = jnp.concatenate([arriving[-half:], expiring[-half:]], 1)
    above = lax.ppermute(tail, axes, [(i, i + 1) for i in range(count - 1)])
    below = lax.ppermute(head, axes, [(i + 1, i) for i in range(count - 1)])
    whole = pl.BlockSpec(memory_space=pltpu.VMEM)
    return pl.pallas_call(
        filter_kernel,
        in_specs=[pl.BlockSpec(memory_space=pltpu.SMEM), whole, whole, whole, whole],
        out_specs=whole,
        out_shape=jax.ShapeDtypeStruct((stripe, 2 * samples), BF16),
        scratch_shapes=[pltpu.VMEM((stripe + 16, 2 * samples), F32)],
        name="filter_stripe",
    )(taps, arriving, expiring, above, below)


def basis_kernel(block, gram, vectors, out, work):
    count = gram.shape[0]
    work[...] = gram[...]
    down = lax.broadcasted_iota(jnp.int32, (block, block), 0)
    across = lax.broadcasted_iota(jnp.int32, (block, block), 1)
    lane = lax.broadcasted_iota(jnp.int32, (1, count), 1)
    for start in range(0, count, block):
        end = start + block
        strip = work[start:end, :]
        square = strip[:, start:end]
        for j in range(block):
            row = square[j : j + 1, :]
            ratio = jnp.where(down[:, :1] > j, square[:, j : j + 1] / row[:, j : j + 1], 0.0)
            row = jnp.where(across[:1] == j, 1.0, row)
            square = jnp.where((across == j) & (down > j), 0.0, square) - ratio * row
        pivot = jnp.sum(jnp.where(down == across, square, 0.0), axis=1, keepdims=True)
        inverse = lax.rsqrt(pivot) * jnp.where(
            down > across, square, jnp.where(down == across, 1.0, 0.0)
        )
        strip = jnp.dot(inverse, strip, precision=HIGHEST, preferred_element_type=F32)
        pieces = [strip[:, :start]] if start else []
        pieces.append(inverse)
        if end < count:
            pieces.append(strip[:, end:])
        done = jnp.concatenate(pieces, axis=1)
        work[start:end, :] = done
        if end < count:
            change = lax.dot_general(
                strip[:, end:],
                done,
                (((0,), (0,)), ((), ())),
                precision=HIGHEST,
                preferred_element_type=F32,
            )
            old = jnp.where((lane >= start) & (lane < end), 0.0, work[end:, :])
            work[end:, :] = old - change
    down = lax.broadcasted_iota(jnp.int32, (count, count), 0)
    across = lax.broadcasted_iota(jnp.int32, (count, count), 1)
    factor = jnp.where(down >= across, work[...], 0.0)
    out[...] = lax.dot_general(
        vectors[...],
        factor,
        (((1,), (1,)), ((), ())),
        precision=HIGHEST,
        preferred_element_type=F32,
    )


def normalized(gram, vectors):
    count = gram.shape[0]
    return pl.pallas_call(
        functools.partial(basis_kernel, min(count, 64)),
        out_shape=jax.ShapeDtypeStruct(vectors.shape, F32),
        scratch_shapes=[pltpu.VMEM((count, count), F32)],
        compiler_params=pltpu.CompilerParams(vmem_limit_bytes=VMEM_LIMIT),
        name="normalized",
    )(gram, vectors)


def negated(data, samples):
    return jnp.concatenate([data[:, :samples], -data[:, samples:]], 1)


def inner(data, values):
    return lax.dot_general(data.astype(F32), values, (((0,), (0,)), ((), ())), precision=HIGHEST)


def correction(data, sums):
    high, low = halves(sums)
    return jnp.dot(data, high, preferred_element_type=F32) + jnp.dot(
        data, low, preferred_element_type=F32
    )


def shards(arriving, expiring, taps, covariance, vectors):
    stripe, samples = arriving.shape
    kept = vectors.shape[1]
    count_row, count_col = lax.axis_size("row"), lax.axis_size("col")
    channels = stripe * count_row * count_col
    planes = count_row // 2
    row_index, col_index = lax.axis_index("row"), lax.axis_index("col")
    z, x = row_index // 2, row_index % 2
    scale = 1.0 / samples

    own = jnp.concatenate(halves(vectors.T), 0)
    blocks = gather_pairs(own, "col")

    largest = largest_everywhere(jnp.max(jnp.abs(vectors)), planes)
    limit = 2.0 * 6.0 * channels
    grown = room(limit)
    size = power_of_two_for(largest[0, 0]) * grown

    filtered = filter_stripe(arriving, expiring, taps)
    moves = []
    for source in range(count_row * count_col):
        moves.append((source, (source % count_row) * count_col + source // count_row))
    other_filtered = lax.ppermute(filtered, ("row", "col"), moves)
    row_filtered = lax.all_gather(filtered, "col", axis=0, tiled=True)
    column_filtered = lax.all_gather(other_filtered, "row", axis=0, tiled=True)

    share = 1.0 / 16.0
    extra = turned(scatter_sum(inner(negated(filtered, samples), vectors) * share))
    received = []
    for j in reversed(range(planes)):
        if j == max(planes - 2, 0):
            extra = after(extra, other_filtered)
        send, keep = first_part(blocks, covariance, extra, z ^ j, x, col_index, stripe)
        half_sum = keep * size + swap((send * size).astype(F16), "row", 1).astype(F32)
        if j:
            received.append(swap(half_sum.astype(F16), "row", 2 * j))
        else:
            received.append(half_sum)
    total = received[-1]
    for part in received[:-1]:
        total = total + part.astype(F32)
    total = turned(total * (1.0 / grown))
    first_inner = gather_parts(total[stripe:] * (scale / share))
    first = total[:stripe] + correction(other_filtered, first_inner)

    grown = room(2.0 * (6.0 + 2.0 * (taps.shape[0] * 1.4 * 0.6) ** 2) * channels)
    own = (first * grown).astype(F16)
    far = [own] + [swap(own, "row", 2 * j) for j in range(1, planes)]
    partial, partials = None, []
    for j in range(planes):
        sent = far[j] if j < 2 else after(far[j], partials[j - 2])
        beside = swap(sent, "row", 1)
        entries = []
        for payload in (far[j], beside):
            own_entries = j == 0 and payload is own
            entries += halves(first if own_entries else payload.astype(F32) * (1.0 / grown))
        partial = second_part(covariance, entries, z ^ j, x, partial)
        partials.append(partial)
    second_inner = scatter_sum(inner(negated(other_filtered, samples), first) * scale)
    for mask, earlier in zip(bits_of("row"), partials):
        second_inner = second_inner + swap(after(second_inner, earlier), "row", mask)
    second_inner = gather_parts(second_inner)

    cells = partial.reshape(count_col, stripe, kept)
    for mask in bits_of("col"):
        cells = cells.reshape(cells.shape[0] // 2, 2, stripe, kept)
        upper = is_set("col", mask)
        mine = pick(upper, cells[:, 0], cells[:, 1])
        send = pick(upper, cells[:, 1], cells[:, 0])
        if mask == 1:
            cells = mine + swap(send, "col", mask)
        else:
            power = power_of_two_for(jnp.max(jnp.abs(send)))
            tail = jnp.full(send.shape[:1] + (16, kept), jnp.log2(power))
            payload = jnp.concatenate([send * (power * room(2.0)), tail], 1).astype(F16)
            other = swap(payload, "col", mask).astype(F32)
            power = lax.reduce_precision(jnp.exp2(-jnp.round(other[:, stripe : stripe + 1])), 8, 3)
            cells = mine + other[:, :stripe] * (power * (1.0 / room(2.0)))
    second = cells.reshape(stripe, kept) + correction(filtered, second_inner)
    gram_part = inner(second, second)

    signed_rows = negated(after(row_filtered, partials[max(planes - 3, 0)]), samples)
    updated = None
    for part in range(4):
        updated = update_part(
            covariance, signed_rows, column_filtered, part, 4, updated, scale
        )
    gram = gather_parts(sum_over_row(scatter_sum(gram_part))) / channels
    basis = normalized(after(gram, updated), second)
    return (updated, basis)


def solution(mesh):
    in_specs = (
        P(("row", "col"), None),
        P(("row", "col"), None),
        P(),
        P("row", "col"),
        P(("row", "col"), None),
    )
    out_specs = (P("row", "col"), P(("row", "col"), None))
    return jax.shard_map(shards, mesh=mesh, in_specs=in_specs, out_specs=out_specs, check_vma=False)
```

```python
import functools
import math

import jax
import jax.numpy as jnp
from jax import lax
from jax.experimental import pallas as pl
from jax.experimental.pallas import tpu as pltpu
from jax.sharding import PartitionSpec as P

HIGHEST = lax.Precision.HIGHEST
F32, F16, BF16 = jnp.float32, jnp.float16, jnp.bfloat16
VMEM_LIMIT = 40 * 1024 * 1024


def swap(cells, axis, mask):
    return lax.ppermute(cells, axis, [(i, i ^ mask) for i in range(lax.axis_size(axis))])


def bits_of(axis):
    return [1 << b for b in range(lax.axis_size(axis).bit_length() - 1)]


def is_set(axis, mask):
    return (lax.axis_index(axis) & mask) != 0


def pick(upper, first, second):
    return jnp.where(upper, second, first)


def room(bound):
    return 2.0 ** (15 - math.ceil(math.log2(bound)))


def power_of_two_for(value):
    exponent = jnp.floor(jnp.log2(jnp.maximum(value, 1e-30)))
    return lax.reduce_precision(jnp.exp2(-exponent - 1.0), 8, 3)


def after(values, earlier):
    corner = lax.slice(earlier, (0,) * earlier.ndim, (1,) * earlier.ndim)
    entry = corner.reshape(()).astype(F32)
    return values + jnp.where(jnp.isnan(entry), 1, 0).astype(values.dtype)


def gather_pairs(cells, axis):
    blocks = {0: cells}
    for mask in reversed(bits_of(axis)):
        for known in list(blocks):
            blocks[known | mask] = swap(blocks[known], axis, mask)
    return [blocks[mask] for mask in range(lax.axis_size(axis))]


def scatter_sum(cells):
    for mask in bits_of("col"):
        half = cells.shape[0] // 2
        upper = is_set("col", mask)
        low, high = cells[:half], cells[half:]
        cells = pick(upper, low, high) + swap(pick(upper, high, low), "col", mask)
    return cells


def sum_over_row(cells):
    for mask in bits_of("row"):
        cells = cells + swap(cells, "row", mask)
    return cells


def gather_parts(cells):
    for mask in reversed(bits_of("col")):
        other = swap(cells, "col", mask)
        upper = is_set("col", mask)
        cells = jnp.concatenate([pick(upper, cells, other), pick(upper, other, cells)], 0)
    return cells


def largest_everywhere(value, planes):
    value = jnp.full((8, 128), value)
    for other in [swap(value, "row", 2 * j) for j in range(1, planes)]:
        value = jnp.maximum(value, other)
    value = jnp.maximum(value, swap(value, "row", 1))
    for mask in bits_of("col"):
        value = jnp.maximum(value, swap(value, "col", mask))
    return value


def halves(values):
    high = lax.reduce_precision(values, 8, 7)
    return high.astype(BF16), (values - high).astype(BF16)


def split(values):
    high = values.astype(BF16)
    return high, (values - high.astype(F32)).astype(BF16)


def first_kernel(blocks, place, *refs):
    extra, refs = refs[0], refs[1:]
    vectors, tiles = refs[:blocks], refs[blocks : 2 * blocks]
    send, keep = refs[-2:]
    count = send.shape[0]
    total = None
    for part, tile in zip(vectors, tiles):
        high, low = split(tile[...])
        both = jnp.dot(part[...], high, preferred_element_type=F32)
        rest = jnp.dot(part[:count], low, preferred_element_type=F32)
        term = both[:count] + both[count:] + rest
        total = term if total is None else total + term

    @pl.when(pl.program_id(0) == 0)
    def _():
        send[:, : total.shape[1]] = total
        send[:, total.shape[1] :] = extra[...]

    @pl.when(pl.program_id(0) == 1)
    def _():
        keep[:, : total.shape[1]] = total
        keep[:, total.shape[1] :] = extra[...]


def first_part(vectors, tile, extra, z, x, column, stripe, waits=()):
    rows = tile.shape[0]
    blocks = len(vectors)
    count = vectors[0].shape[0] // 2
    depth = rows // blocks
    width = extra.shape[1]
    if stripe % 128:
        return first_part_plain(vectors, tile, extra, z, x, column, stripe)
    place = jnp.stack(
        [z * 2 + (1 - x), z * 2 + x] + [column ^ i for i in range(blocks)]
    ).astype(jnp.int32)

    def rows_of(member):
        return lambda i, p: (p[2 + member], p[i])

    shape = (count, stripe + width)
    return pl.pallas_call(
        functools.partial(first_kernel, blocks),
        grid_spec=pltpu.PrefetchScalarGridSpec(
            num_scalar_prefetch=1,
            grid=(2,),
            in_specs=[pl.BlockSpec((count, width), lambda i, p: (0, 0))]
            + [pl.BlockSpec((2 * count, depth), lambda i, p: (0, 0))] * blocks
            + [pl.BlockSpec((depth, stripe), rows_of(i)) for i in range(blocks)]
            + [pl.BlockSpec(memory_space=pl.ANY)] * len(waits),
            out_specs=[pl.BlockSpec(shape, lambda i, p: (0, 0))] * 2,
        ),
        out_shape=[jax.ShapeDtypeStruct(shape, F32)] * 2,
        compiler_params=pltpu.CompilerParams(vmem_limit_bytes=VMEM_LIMIT),
        cost_estimate=pl.CostEstimate(
            flops=12 * count * rows * stripe, bytes_accessed=8 * rows * stripe, transcendentals=0
        ),
        name="first_part",
    )(place, extra, *vectors, *([tile] * blocks), *waits)


def first_part_plain(vectors, tile, extra, z, x, column, stripe):
    count = vectors[0].shape[0] // 2
    depth = tile.shape[0] // len(vectors)
    results = []
    for other in (1 - x, x):
        total = 0.0
        for i, part in enumerate(vectors):
            start = ((column ^ i) * depth, (z * 2 + other) * stripe)
            cells = lax.dynamic_slice(tile, start, (depth, stripe))
            values = part[:count].astype(F32) + part[count:].astype(F32)
            total = total + jnp.dot(values, cells, precision=HIGHEST)
        results.append(jnp.concatenate([total, extra], 1))
    return results


def second_part_plain(tile, entries, z, x, before):
    depth = entries[0].shape[0]
    total = 0.0 if before is None else before
    for i, other in enumerate((x, 1 - x)):
        start = (0, (z * 2 + other) * depth)
        cells = lax.dynamic_slice(tile, start, (tile.shape[0], depth))
        values = entries[2 * i].astype(F32) + entries[2 * i + 1].astype(F32)
        total = total + jnp.dot(cells, values, precision=HIGHEST)
    return total


def turn_kernel(cells, out):
    out[...] = cells[...].T


def turned(cells):
    return pl.pallas_call(
        turn_kernel,
        out_shape=jax.ShapeDtypeStruct(cells.shape[::-1], F32),
        compiler_params=pltpu.CompilerParams(vmem_limit_bytes=VMEM_LIMIT),
        name="turned",
    )(cells)


def second_kernel(started, place, *refs):
    tiles, entries = refs[:2], refs[2:6]
    out = refs[-1]
    total = refs[6][...] if started else None
    for tile, top, rest in zip(tiles, entries[::2], entries[1::2]):
        high, low = split(tile[...])
        term = (
            jnp.dot(high, top[...], preferred_element_type=F32)
            + jnp.dot(high, rest[...], preferred_element_type=F32)
            + jnp.dot(low, top[...], preferred_element_type=F32)
        )
        total = term if total is None else total + term
    out[...] = total


def second_part(tile, entries, z, x, before, waits=()):
    rows = tile.shape[0]
    depth, count = entries[0].shape
    if depth % 128:
        return second_part_plain(tile, entries, z, x, before)
    block = min(rows, 512)
    specs = [
        pl.BlockSpec((block, depth), lambda i, p: (i, p[0])),
        pl.BlockSpec((block, depth), lambda i, p: (i, p[1])),
    ] + [pl.BlockSpec((depth, count), lambda i, p: (0, 0))] * 4
    operands = [tile, tile, *entries]
    total = pl.BlockSpec((block, count), lambda i, p: (i, 0))
    if before is not None:
        specs.append(total)
        operands.append(before)
    specs += [pl.BlockSpec(memory_space=pl.ANY)] * len(waits)
    operands += waits
    return pl.pallas_call(
        functools.partial(second_kernel, before is not None),
        grid_spec=pltpu.PrefetchScalarGridSpec(
            num_scalar_prefetch=1, grid=(rows // block,), in_specs=specs, out_specs=total
        ),
        out_shape=jax.ShapeDtypeStruct((rows, count), F32),
        compiler_params=pltpu.CompilerParams(vmem_limit_bytes=VMEM_LIMIT),
        cost_estimate=pl.CostEstimate(
            flops=12 * count * rows * depth, bytes_accessed=8 * rows * depth, transcendentals=0
        ),
        name="second_part",
    )(jnp.stack([z * 2 + x, z * 2 + (1 - x)]).astype(jnp.int32), *operands)


def update_kernel(scale, tile, rows, columns, *rest):
    change = lax.dot_general(
        rows[...], columns[...], (((1,), (1,)), ((), ())), preferred_element_type=F32
    )
    rest[-2][...] = tile[...] + change * scale
    rest[-1][...] = jnp.zeros(rest[-1].shape, F32)


def update_part(tile, rows, columns, part, parts, before, scale, kept, waits):
    height, width = tile.shape
    depth = rows.shape[1]
    high = min(height // parts, 256)
    steps = height // parts // high
    specs = [
        pl.BlockSpec((high, width), lambda i: (part * steps + i, 0)),
        pl.BlockSpec((high, depth), lambda i: (part * steps + i, 0)),
        pl.BlockSpec((width, depth), lambda i: (0, 0)),
    ]
    operands = [tile, rows, columns]
    if before is not None:
        specs.append(pl.BlockSpec(memory_space=pl.ANY))
        operands.append(before)
    specs += [pl.BlockSpec(memory_space=pl.ANY)] * len(waits)
    operands += waits
    return pl.pallas_call(
        functools.partial(update_kernel, scale),
        grid=(steps,),
        in_specs=specs,
        out_specs=[
            pl.BlockSpec((high, width), lambda i: (part * steps + i, 0)),
            pl.BlockSpec((1, kept), lambda i: (0, 0)),
        ],
        out_shape=[
            jax.ShapeDtypeStruct((height, width), F32),
            jax.ShapeDtypeStruct((1, kept), F32),
        ],
        input_output_aliases={} if before is None else {3: 0},
        compiler_params=pltpu.CompilerParams(vmem_limit_bytes=VMEM_LIMIT),
        cost_estimate=pl.CostEstimate(
            flops=2 * height * width * depth // parts,
            bytes_accessed=8 * height * width // parts,
            transcendentals=0,
        ),
        name="update_part",
    )(*operands)


def filter_kernel(taps, arriving, expiring, above, below, out, work):
    stripe, samples = arriving.shape
    count = taps.shape[0]
    half = count // 2
    work[8 - half : 8, :] = above[...]
    work[8 : 8 + stripe, :samples] = arriving[...]
    work[8 : 8 + stripe, samples:] = expiring[...]
    work[8 + stripe : 8 + stripe + half, :] = below[...]
    step = 64
    for start in range(0, stripe, step):
        total = taps[0] * work[8 - half + start : 8 - half + start + step, :]
        for tap in range(1, count):
            begin = 8 - half + start + tap
            total = total + taps[tap] * work[begin : begin + step, :]
        out[start : start + step, :] = total.astype(BF16)


def filter_stripe(arriving, expiring, taps):
    stripe, samples = arriving.shape
    half = taps.shape[0] // 2
    axes = ("row", "col")
    count = lax.axis_size("row") * lax.axis_size("col")
    head = jnp.concatenate([arriving[:half], expiring[:half]], 1)
    tail = jnp.concatenate([arriving[-half:], expiring[-half:]], 1)
    above = lax.ppermute(tail, axes, [(i, i + 1) for i in range(count - 1)])
    below = lax.ppermute(head, axes, [(i + 1, i) for i in range(count - 1)])
    whole = pl.BlockSpec(memory_space=pltpu.VMEM)
    return pl.pallas_call(
        filter_kernel,
        in_specs=[pl.BlockSpec(memory_space=pltpu.SMEM), whole, whole, whole, whole],
        out_specs=whole,
        out_shape=jax.ShapeDtypeStruct((stripe, 2 * samples), BF16),
        scratch_shapes=[pltpu.VMEM((stripe + 16, 2 * samples), F32)],
        name="filter_stripe",
    )(taps, arriving, expiring, above, below)


def basis_kernel(block, gram, vectors, out, work):
    count = gram.shape[0]
    work[...] = gram[...]
    down = lax.broadcasted_iota(jnp.int32, (block, block), 0)
    across = lax.broadcasted_iota(jnp.int32, (block, block), 1)
    lane = lax.broadcasted_iota(jnp.int32, (1, count), 1)
    for start in range(0, count, block):
        end = start + block
        strip = work[start:end, :]
        square = strip[:, start:end]
        for j in range(block):
            row = square[j : j + 1, :]
            ratio = jnp.where(down[:, :1] > j, square[:, j : j + 1] / row[:, j : j + 1], 0.0)
            row = jnp.where(across[:1] == j, 1.0, row)
            square = jnp.where((across == j) & (down > j), 0.0, square) - ratio * row
        pivot = jnp.sum(jnp.where(down == across, square, 0.0), axis=1, keepdims=True)
        inverse = lax.rsqrt(pivot) * jnp.where(
            down > across, square, jnp.where(down == across, 1.0, 0.0)
        )
        strip = jnp.dot(inverse, strip, precision=HIGHEST, preferred_element_type=F32)
        pieces = [strip[:, :start]] if start else []
        pieces.append(inverse)
        if end < count:
            pieces.append(strip[:, end:])
        done = jnp.concatenate(pieces, axis=1)
        work[start:end, :] = done
        if end < count:
            change = lax.dot_general(
                strip[:, end:],
                done,
                (((0,), (0,)), ((), ())),
                precision=HIGHEST,
                preferred_element_type=F32,
            )
            old = jnp.where((lane >= start) & (lane < end), 0.0, work[end:, :])
            work[end:, :] = old - change
    down = lax.broadcasted_iota(jnp.int32, (count, count), 0)
    across = lax.broadcasted_iota(jnp.int32, (count, count), 1)
    factor = jnp.where(down >= across, work[...], 0.0)
    out[...] = lax.dot_general(
        vectors[...],
        factor,
        (((1,), (1,)), ((), ())),
        precision=HIGHEST,
        preferred_element_type=F32,
    )


def normalized(gram, vectors):
    count = gram.shape[0]
    return pl.pallas_call(
        functools.partial(basis_kernel, min(count, 64)),
        out_shape=jax.ShapeDtypeStruct(vectors.shape, F32),
        scratch_shapes=[pltpu.VMEM((count, count), F32)],
        compiler_params=pltpu.CompilerParams(vmem_limit_bytes=VMEM_LIMIT),
        name="normalized",
    )(gram, vectors)


def negated(data, samples):
    return jnp.concatenate([data[:, :samples], -data[:, samples:]], 1)


def inner(data, values):
    return lax.dot_general(data.astype(F32), values, (((0,), (0,)), ((), ())), precision=HIGHEST)


def correction(data, sums):
    high, low = halves(sums)
    return jnp.dot(data, high, preferred_element_type=F32) + jnp.dot(
        data, low, preferred_element_type=F32
    )


def shards(arriving, expiring, taps, covariance, vectors):
    stripe, samples = arriving.shape
    kept = vectors.shape[1]
    count_row, count_col = lax.axis_size("row"), lax.axis_size("col")
    channels = stripe * count_row * count_col
    planes = count_row // 2
    row_index, col_index = lax.axis_index("row"), lax.axis_index("col")
    z, x = row_index // 2, row_index % 2
    scale = 1.0 / samples

    own = jnp.concatenate(halves(vectors.T), 0)
    blocks = gather_pairs(own, "col")

    largest = largest_everywhere(jnp.max(jnp.abs(vectors)), planes)
    limit = 2.0 * 6.0 * channels
    grown = room(limit)
    size = power_of_two_for(largest[0, 0]) * grown

    filtered = filter_stripe(arriving, expiring, taps)
    moves = []
    for source in range(count_row * count_col):
        moves.append((source, (source % count_row) * count_col + source // count_row))
    other_filtered = lax.ppermute(filtered, ("row", "col"), moves)
    row_filtered = lax.all_gather(filtered, "col", axis=0, tiled=True)
    column_filtered = lax.all_gather(other_filtered, "row", axis=0, tiled=True)

    share = 1.0 / 16.0
    extra = turned(scatter_sum(inner(negated(filtered, samples), vectors) * share))
    received = []
    for j in reversed(range(planes)):
        waits = {0: [other_filtered], 3: received[:1]}.get(len(received), [])
        send, keep = first_part(blocks, covariance, extra, z ^ j, x, col_index, stripe, waits)
        half_sum = keep * size + swap((send * size).astype(F16), "row", 1).astype(F32)
        if j:
            received.append(swap(half_sum.astype(F16), "row", 2 * j).astype(F32))
        else:
            received.append(half_sum)
    total = received[-1]
    for part in received[:-1]:
        total = total + part
    total = turned(total * (1.0 / grown))
    first_inner = gather_parts(total[stripe:] * (scale / share))
    first = total[:stripe] + correction(other_filtered, first_inner)

    grown = room(2.0 * (6.0 + 2.0 * (taps.shape[0] * 1.4 * 0.6) ** 2) * channels)
    own = (first * grown).astype(F16)
    far = [own] + [swap(own, "row", 2 * j) for j in range(1, planes)]
    partial, partials = None, []
    for j in range(planes):
        sent = far[j] if j < 2 else after(far[j], partials[j - 2])
        beside = swap(sent, "row", 1)
        entries = []
        for payload in (far[j], beside):
            own_entries = j == 0 and payload is own
            entries += halves(first if own_entries else payload.astype(F32) * (1.0 / grown))
        waits = [column_filtered] if j == 1 else []
        partial = second_part(covariance, entries, z ^ j, x, partial, waits)
        partials.append(partial)
    second_inner = scatter_sum(inner(negated(other_filtered, samples), first) * scale)
    for mask, earlier in zip(bits_of("row"), partials):
        second_inner = second_inner + swap(after(second_inner, earlier), "row", mask)

    signed_rows = negated(row_filtered, samples)
    updated, written = None, []
    for part, waits in enumerate(([partial], [partial], [partial], [partial])):
        updated, row = update_part(
            covariance, signed_rows, column_filtered, part, 4, updated, scale, kept, waits
        )
        written.append(row)
    second_inner = gather_parts(second_inner + written[0])

    cells = partial.reshape(count_col, stripe, kept)
    for mask in bits_of("col"):
        cells = cells.reshape(cells.shape[0] // 2, 2, stripe, kept)
        upper = is_set("col", mask)
        mine = pick(upper, cells[:, 0], cells[:, 1])
        send = pick(upper, cells[:, 1], cells[:, 0])
        if mask == 1:
            cells = mine + swap(send, "col", mask)
        else:
            power = power_of_two_for(jnp.max(jnp.abs(send)))
            tail = jnp.full(send.shape[:1] + (16, kept), jnp.log2(power))
            payload = jnp.concatenate([send * (power * room(2.0)), tail], 1).astype(F16)
            other = swap(payload, "col", mask).astype(F32)
            power = lax.reduce_precision(jnp.exp2(-jnp.round(other[:, stripe : stripe + 1])), 8, 3)
            cells = mine + other[:, :stripe] * (power * (1.0 / room(2.0)))
    second = cells.reshape(stripe, kept) + correction(filtered, second_inner) + written[1]

    gram = scatter_sum(inner(second, second))
    for i, mask in enumerate(bits_of("row")):
        gram = gram + swap(gram, "row", mask)
        if i < 2:
            gram = gram + written[2 + i]
    basis = normalized(gather_parts(gram) / channels, second)
    return (updated, basis)


def solution(mesh):
    in_specs = (
        P(("row", "col"), None),
        P(("row", "col"), None),
        P(),
        P("row", "col"),
        P(("row", "col"), None),
    )
    out_specs = (P("row", "col"), P(("row", "col"), None))
    return jax.shard_map(shards, mesh=mesh, in_specs=in_specs, out_specs=out_specs, check_vma=False)
```

```python
import functools
import math

import jax
import jax.numpy as jnp
from jax import lax
from jax.experimental import pallas as pl
from jax.experimental.pallas import tpu as pltpu
from jax.sharding import PartitionSpec as P

HIGHEST = lax.Precision.HIGHEST
F32, F16, BF16 = jnp.float32, jnp.float16, jnp.bfloat16
VMEM_LIMIT = 40 * 1024 * 1024


def swap(cells, axis, mask):
    return lax.ppermute(cells, axis, [(i, i ^ mask) for i in range(lax.axis_size(axis))])


def bits_of(axis):
    return [1 << b for b in range(lax.axis_size(axis).bit_length() - 1)]


def is_set(axis, mask):
    return (lax.axis_index(axis) & mask) != 0


def pick(upper, first, second):
    return jnp.where(upper, second, first)


def room(bound):
    return 2.0 ** (15 - math.ceil(math.log2(bound)))


def power_of_two_for(value):
    exponent = jnp.floor(jnp.log2(jnp.maximum(value, 1e-30)))
    return lax.reduce_precision(jnp.exp2(-exponent - 1.0), 8, 3)


def after(values, earlier):
    corner = lax.slice(earlier, (0,) * earlier.ndim, (1,) * earlier.ndim)
    entry = corner.reshape(()).astype(F32)
    return values + jnp.where(jnp.isnan(entry), 1, 0).astype(values.dtype)


def gather_pairs(cells, axis):
    blocks = {0: cells}
    for mask in reversed(bits_of(axis)):
        for known in list(blocks):
            blocks[known | mask] = swap(blocks[known], axis, mask)
    return [blocks[mask] for mask in range(lax.axis_size(axis))]


def scatter_sum(cells):
    for mask in bits_of("col"):
        half = cells.shape[0] // 2
        upper = is_set("col", mask)
        low, high = cells[:half], cells[half:]
        cells = pick(upper, low, high) + swap(pick(upper, high, low), "col", mask)
    return cells


def sum_over_row(cells):
    for mask in bits_of("row"):
        cells = cells + swap(cells, "row", mask)
    return cells


def gather_parts(cells):
    for mask in reversed(bits_of("col")):
        other = swap(cells, "col", mask)
        upper = is_set("col", mask)
        cells = jnp.concatenate([pick(upper, cells, other), pick(upper, other, cells)], 0)
    return cells


def largest_everywhere(value, planes):
    value = jnp.full((8, 128), value)
    for other in [swap(value, "row", 2 * j) for j in range(1, planes)]:
        value = jnp.maximum(value, other)
    value = jnp.maximum(value, swap(value, "row", 1))
    for mask in bits_of("col"):
        value = jnp.maximum(value, swap(value, "col", mask))
    return value


def halves(values):
    high = lax.reduce_precision(values, 8, 7)
    return high.astype(BF16), (values - high).astype(BF16)


def split(values):
    high = values.astype(BF16)
    return high, (values - high.astype(F32)).astype(BF16)


def first_kernel(blocks, place, *refs):
    extra, refs = refs[0], refs[1:]
    vectors, tiles = refs[:blocks], refs[blocks : 2 * blocks]
    send, keep = refs[-2:]
    count = send.shape[0]
    total = None
    for part, tile in zip(vectors, tiles):
        high, low = split(tile[...])
        both = jnp.dot(part[...], high, preferred_element_type=F32)
        rest = jnp.dot(part[:count], low, preferred_element_type=F32)
        term = both[:count] + both[count:] + rest
        total = term if total is None else total + term

    @pl.when(pl.program_id(0) == 0)
    def _():
        send[:, : total.shape[1]] = total
        send[:, total.shape[1] :] = extra[...]

    @pl.when(pl.program_id(0) == 1)
    def _():
        keep[:, : total.shape[1]] = total
        keep[:, total.shape[1] :] = extra[...]


def first_part(vectors, tile, extra, z, x, column, stripe, waits=()):
    rows = tile.shape[0]
    blocks = len(vectors)
    count = vectors[0].shape[0] // 2
    depth = rows // blocks
    width = extra.shape[1]
    if stripe % 128:
        return first_part_plain(vectors, tile, extra, z, x, column, stripe)
    place = jnp.stack(
        [z * 2 + (1 - x), z * 2 + x] + [column ^ i for i in range(blocks)]
    ).astype(jnp.int32)

    def rows_of(member):
        return lambda i, p: (p[2 + member], p[i])

    shape = (count, stripe + width)
    return pl.pallas_call(
        functools.partial(first_kernel, blocks),
        grid_spec=pltpu.PrefetchScalarGridSpec(
            num_scalar_prefetch=1,
            grid=(2,),
            in_specs=[pl.BlockSpec((count, width), lambda i, p: (0, 0))]
            + [pl.BlockSpec((2 * count, depth), lambda i, p: (0, 0))] * blocks
            + [pl.BlockSpec((depth, stripe), rows_of(i)) for i in range(blocks)]
            + [pl.BlockSpec(memory_space=pl.ANY)] * len(waits),
            out_specs=[pl.BlockSpec(shape, lambda i, p: (0, 0))] * 2,
        ),
        out_shape=[jax.ShapeDtypeStruct(shape, F32)] * 2,
        compiler_params=pltpu.CompilerParams(vmem_limit_bytes=VMEM_LIMIT),
        cost_estimate=pl.CostEstimate(
            flops=12 * count * rows * stripe, bytes_accessed=8 * rows * stripe, transcendentals=0
        ),
        name="first_part",
    )(place, extra, *vectors, *([tile] * blocks), *waits)


def first_part_plain(vectors, tile, extra, z, x, column, stripe):
    count = vectors[0].shape[0] // 2
    depth = tile.shape[0] // len(vectors)
    results = []
    for other in (1 - x, x):
        total = 0.0
        for i, part in enumerate(vectors):
            start = ((column ^ i) * depth, (z * 2 + other) * stripe)
            cells = lax.dynamic_slice(tile, start, (depth, stripe))
            values = part[:count].astype(F32) + part[count:].astype(F32)
            total = total + jnp.dot(values, cells, precision=HIGHEST)
        results.append(jnp.concatenate([total, extra], 1))
    return results


def second_part_plain(tile, entries, z, x, before):
    depth = entries[0].shape[0]
    total = 0.0 if before is None else before
    for i, other in enumerate((x, 1 - x)):
        start = (0, (z * 2 + other) * depth)
        cells = lax.dynamic_slice(tile, start, (tile.shape[0], depth))
        values = entries[2 * i].astype(F32) + entries[2 * i + 1].astype(F32)
        total = total + jnp.dot(cells, values, precision=HIGHEST)
    return total


def turn_kernel(cells, out):
    out[...] = cells[...].T


def turned(cells):
    return pl.pallas_call(
        turn_kernel,
        out_shape=jax.ShapeDtypeStruct(cells.shape[::-1], F32),
        compiler_params=pltpu.CompilerParams(vmem_limit_bytes=VMEM_LIMIT),
        name="turned",
    )(cells)


def second_kernel(started, place, *refs):
    tiles, entries = refs[:2], refs[2:6]
    out = refs[-1]
    total = refs[6][...] if started else None
    for tile, top, rest in zip(tiles, entries[::2], entries[1::2]):
        high, low = split(tile[...])
        term = (
            jnp.dot(high, top[...], preferred_element_type=F32)
            + jnp.dot(high, rest[...], preferred_element_type=F32)
            + jnp.dot(low, top[...], preferred_element_type=F32)
        )
        total = term if total is None else total + term
    out[...] = total


def second_part(tile, entries, z, x, before, waits=()):
    rows = tile.shape[0]
    depth, count = entries[0].shape
    if depth % 128:
        return second_part_plain(tile, entries, z, x, before)
    block = min(rows, 512)
    specs = [
        pl.BlockSpec((block, depth), lambda i, p: (i, p[0])),
        pl.BlockSpec((block, depth), lambda i, p: (i, p[1])),
    ] + [pl.BlockSpec((depth, count), lambda i, p: (0, 0))] * 4
    operands = [tile, tile, *entries]
    total = pl.BlockSpec((block, count), lambda i, p: (i, 0))
    if before is not None:
        specs.append(total)
        operands.append(before)
    specs += [pl.BlockSpec(memory_space=pl.ANY)] * len(waits)
    operands += waits
    return pl.pallas_call(
        functools.partial(second_kernel, before is not None),
        grid_spec=pltpu.PrefetchScalarGridSpec(
            num_scalar_prefetch=1, grid=(rows // block,), in_specs=specs, out_specs=total
        ),
        out_shape=jax.ShapeDtypeStruct((rows, count), F32),
        compiler_params=pltpu.CompilerParams(vmem_limit_bytes=VMEM_LIMIT),
        cost_estimate=pl.CostEstimate(
            flops=12 * count * rows * depth, bytes_accessed=8 * rows * depth, transcendentals=0
        ),
        name="second_part",
    )(jnp.stack([z * 2 + x, z * 2 + (1 - x)]).astype(jnp.int32), *operands)


def update_kernel(scale, tile, rows, columns, *rest):
    change = lax.dot_general(
        rows[...], columns[...], (((1,), (1,)), ((), ())), preferred_element_type=F32
    )
    rest[-2][...] = tile[...] + change * scale
    rest[-1][...] = jnp.zeros(rest[-1].shape, F32)


def update_part(tile, rows, columns, part, parts, before, scale, kept, waits):
    height, width = tile.shape
    depth = rows.shape[1]
    high = min(height // parts, 256)
    steps = height // parts // high
    specs = [
        pl.BlockSpec((high, width), lambda i: (part * steps + i, 0)),
        pl.BlockSpec((high, depth), lambda i: (part * steps + i, 0)),
        pl.BlockSpec((width, depth), lambda i: (0, 0)),
    ]
    operands = [tile, rows, columns]
    if before is not None:
        specs.append(pl.BlockSpec(memory_space=pl.ANY))
        operands.append(before)
    specs += [pl.BlockSpec(memory_space=pl.ANY)] * len(waits)
    operands += waits
    return pl.pallas_call(
        functools.partial(update_kernel, scale),
        grid=(steps,),
        in_specs=specs,
        out_specs=[
            pl.BlockSpec((high, width), lambda i: (part * steps + i, 0)),
            pl.BlockSpec((1, kept), lambda i: (0, 0)),
        ],
        out_shape=[
            jax.ShapeDtypeStruct((height, width), F32),
            jax.ShapeDtypeStruct((1, kept), F32),
        ],
        input_output_aliases={} if before is None else {3: 0},
        compiler_params=pltpu.CompilerParams(vmem_limit_bytes=VMEM_LIMIT),
        cost_estimate=pl.CostEstimate(
            flops=2 * height * width * depth // parts,
            bytes_accessed=8 * height * width // parts,
            transcendentals=0,
        ),
        name="update_part",
    )(*operands)


def filter_kernel(taps, arriving, expiring, above, below, out, work):
    stripe, samples = arriving.shape
    count = taps.shape[0]
    half = count // 2
    work[8 - half : 8, :] = above[...]
    work[8 : 8 + stripe, :samples] = arriving[...]
    work[8 : 8 + stripe, samples:] = expiring[...]
    work[8 + stripe : 8 + stripe + half, :] = below[...]
    step = 64
    for start in range(0, stripe, step):
        total = taps[0] * work[8 - half + start : 8 - half + start + step, :]
        for tap in range(1, count):
            begin = 8 - half + start + tap
            total = total + taps[tap] * work[begin : begin + step, :]
        out[start : start + step, :] = total.astype(BF16)


def filter_stripe(arriving, expiring, taps):
    stripe, samples = arriving.shape
    half = taps.shape[0] // 2
    axes = ("row", "col")
    count = lax.axis_size("row") * lax.axis_size("col")
    head = jnp.concatenate([arriving[:half], expiring[:half]], 1)
    tail = jnp.concatenate([arriving[-half:], expiring[-half:]], 1)
    above = lax.ppermute(tail, axes, [(i, i + 1) for i in range(count - 1)])
    below = lax.ppermute(head, axes, [(i + 1, i) for i in range(count - 1)])
    whole = pl.BlockSpec(memory_space=pltpu.VMEM)
    return pl.pallas_call(
        filter_kernel,
        in_specs=[pl.BlockSpec(memory_space=pltpu.SMEM), whole, whole, whole, whole],
        out_specs=whole,
        out_shape=jax.ShapeDtypeStruct((stripe, 2 * samples), BF16),
        scratch_shapes=[pltpu.VMEM((stripe + 16, 2 * samples), F32)],
        name="filter_stripe",
    )(taps, arriving, expiring, above, below)


def basis_kernel(block, gram, vectors, out, work):
    count = gram.shape[0]
    work[...] = gram[...]
    down = lax.broadcasted_iota(jnp.int32, (block, block), 0)
    across = lax.broadcasted_iota(jnp.int32, (block, block), 1)
    lane = lax.broadcasted_iota(jnp.int32, (1, count), 1)
    for start in range(0, count, block):
        end = start + block
        strip = work[start:end, :]
        square = strip[:, start:end]
        for j in range(block):
            row = square[j : j + 1, :]
            ratio = jnp.where(down[:, :1] > j, square[:, j : j + 1] / row[:, j : j + 1], 0.0)
            row = jnp.where(across[:1] == j, 1.0, row)
            square = jnp.where((across == j) & (down > j), 0.0, square) - ratio * row
        pivot = jnp.sum(jnp.where(down == across, square, 0.0), axis=1, keepdims=True)
        inverse = lax.rsqrt(pivot) * jnp.where(
            down > across, square, jnp.where(down == across, 1.0, 0.0)
        )
        strip = jnp.dot(inverse, strip, precision=HIGHEST, preferred_element_type=F32)
        pieces = [strip[:, :start]] if start else []
        pieces.append(inverse)
        if end < count:
            pieces.append(strip[:, end:])
        done = jnp.concatenate(pieces, axis=1)
        work[start:end, :] = done
        if end < count:
            change = lax.dot_general(
                strip[:, end:],
                done,
                (((0,), (0,)), ((), ())),
                precision=HIGHEST,
                preferred_element_type=F32,
            )
            old = jnp.where((lane >= start) & (lane < end), 0.0, work[end:, :])
            work[end:, :] = old - change
    down = lax.broadcasted_iota(jnp.int32, (count, count), 0)
    across = lax.broadcasted_iota(jnp.int32, (count, count), 1)
    factor = jnp.where(down >= across, work[...], 0.0)
    out[...] = lax.dot_general(
        vectors[...],
        factor,
        (((1,), (1,)), ((), ())),
        precision=HIGHEST,
        preferred_element_type=F32,
    )


def normalized(gram, vectors):
    count = gram.shape[0]
    return pl.pallas_call(
        functools.partial(basis_kernel, min(count, 64)),
        out_shape=jax.ShapeDtypeStruct(vectors.shape, F32),
        scratch_shapes=[pltpu.VMEM((count, count), F32)],
        compiler_params=pltpu.CompilerParams(vmem_limit_bytes=VMEM_LIMIT),
        name="normalized",
    )(gram, vectors)


def negated(data, samples):
    return jnp.concatenate([data[:, :samples], -data[:, samples:]], 1)


def inner(data, values):
    return lax.dot_general(data.astype(F32), values, (((0,), (0,)), ((), ())), precision=HIGHEST)


def correction(data, sums):
    high, low = halves(sums)
    return jnp.dot(data, high, preferred_element_type=F32) + jnp.dot(
        data, low, preferred_element_type=F32
    )


def shards(arriving, expiring, taps, covariance, vectors):
    stripe, samples = arriving.shape
    kept = vectors.shape[1]
    count_row, count_col = lax.axis_size("row"), lax.axis_size("col")
    channels = stripe * count_row * count_col
    planes = count_row // 2
    row_index, col_index = lax.axis_index("row"), lax.axis_index("col")
    z, x = row_index // 2, row_index % 2
    scale = 1.0 / samples

    own = jnp.concatenate(halves(vectors.T), 0)
    blocks = gather_pairs(own, "col")

    largest = largest_everywhere(jnp.max(jnp.abs(vectors)), planes)
    limit = 2.0 * 6.0 * channels
    grown = room(limit)
    size = power_of_two_for(largest[0, 0]) * grown

    filtered = filter_stripe(arriving, expiring, taps)
    moves = []
    for source in range(count_row * count_col):
        moves.append((source, (source % count_row) * count_col + source // count_row))
    other_filtered = lax.ppermute(filtered, ("row", "col"), moves)
    row_filtered = lax.all_gather(filtered, "col", axis=0, tiled=True)
    column_filtered = lax.all_gather(other_filtered, "row", axis=0, tiled=True)

    share = 1.0 / 16.0
    extra = turned(scatter_sum(inner(negated(filtered, samples), vectors) * share))
    received = []
    for j in reversed(range(planes)):
        waits = {0: [other_filtered], 3: received[:1]}.get(len(received), [])
        send, keep = first_part(blocks, covariance, extra, z ^ j, x, col_index, stripe, waits)
        half_sum = keep * size + swap((send * size).astype(F16), "row", 1).astype(F32)
        if j:
            received.append(swap(half_sum.astype(F16), "row", 2 * j).astype(F32))
        else:
            received.append(half_sum)
    total = received[-1]
    for part in received[:-1]:
        total = total + part
    total = turned(total * (1.0 / grown))
    first_inner = gather_parts(total[stripe:] * (scale / share))
    first = total[:stripe] + correction(other_filtered, first_inner)

    grown = room(2.0 * (6.0 + 2.0 * (taps.shape[0] * 1.4 * 0.6) ** 2) * channels)
    own = (first * grown).astype(F16)
    far = [own] + [swap(own, "row", 2 * j) for j in range(1, planes)]
    partial, partials = None, []
    for j in range(planes):
        sent = far[j] if j < 2 else after(far[j], partials[j - 2])
        beside = swap(sent, "row", 1)
        entries = []
        for payload in (far[j], beside):
            own_entries = j == 0 and payload is own
            entries += halves(first if own_entries else payload.astype(F32) * (1.0 / grown))
        waits = [column_filtered] if j == 1 else []
        partial = second_part(covariance, entries, z ^ j, x, partial, waits)
        partials.append(partial)
    second_inner = scatter_sum(inner(negated(other_filtered, samples), first) * scale)
    for mask, earlier in zip(bits_of("row"), partials):
        second_inner = second_inner + swap(after(second_inner, earlier), "row", mask)

    signed_rows = negated(after(row_filtered, partials[max(planes - 2, 0)]), samples)
    updated, written = None, []
    for part, waits in enumerate(([partial], [partial], [partial], [partial])):
        updated, row = update_part(
            covariance, signed_rows, column_filtered, part, 4, updated, scale, kept, waits
        )
        written.append(row)
    second_inner = gather_parts(second_inner + written[0])

    cells = partial.reshape(count_col, stripe, kept)
    for mask in bits_of("col"):
        cells = cells.reshape(cells.shape[0] // 2, 2, stripe, kept)
        upper = is_set("col", mask)
        mine = pick(upper, cells[:, 0], cells[:, 1])
        send = pick(upper, cells[:, 1], cells[:, 0])
        if mask == 1:
            cells = mine + swap(send, "col", mask)
        else:
            power = power_of_two_for(jnp.max(jnp.abs(send)))
            tail = jnp.full(send.shape[:1] + (16, kept), jnp.log2(power))
            payload = jnp.concatenate([send * (power * room(2.0)), tail], 1).astype(F16)
            other = swap(payload, "col", mask).astype(F32)
            power = lax.reduce_precision(jnp.exp2(-jnp.round(other[:, stripe : stripe + 1])), 8, 3)
            cells = mine + other[:, :stripe] * (power * (1.0 / room(2.0)))
    second = cells.reshape(stripe, kept) + correction(filtered, second_inner) + written[1]

    gram = scatter_sum(inner(second, second))
    for i, mask in enumerate(bits_of("row")):
        gram = gram + swap(gram, "row", mask)
        if i in (0, 2):
            gram = gram + written[2 + i // 2]
    basis = normalized(gather_parts(gram) / channels, second)
    return (updated, basis)


def solution(mesh):
    in_specs = (
        P(("row", "col"), None),
        P(("row", "col"), None),
        P(),
        P("row", "col"),
        P(("row", "col"), None),
    )
    out_specs = (P("row", "col"), P(("row", "col"), None))
    return jax.shard_map(shards, mesh=mesh, in_specs=in_specs, out_specs=out_specs, check_vma=False)
```
